512 devices in a mesh: samp: 64 (over z_hi, y, x), par: 8 (over z_lo, core).
Axes of the slice: x: 4, y: 8, z: 8 (z_hi: 2, z_lo: 4; z = z_hi * 4 + z_lo), core: 2. Of those that a mesh axis runs over, the one named last changes fastest.
Arguments:
- hidden: bfloat16 [64, 256, 1024], P('samp'), may hold values from -6 to 6
- configs: int32 [64, 256], P('samp'), may hold values from 0 to 3
- embed: bfloat16 [4, 1024], replicated, may hold values from -6 to 6
- w_up: bfloat16 [1024, 4096], P(None, 'par'), may hold values from -0.1875 to 0.1875
- readout: float32 [4096], P('par'), may hold values from -6 to 6
- energies: float32 [64], P('samp'), may hold values from -12 to 12
Outputs:
- update: float32 [1024, 4096], P('samp', 'par')
The draws below stay inside these ranges and needn't reach their ends.
All inputs are finite; a program needn't handle non-finite values.
Results may differ from the reference program's by a relative error of at most 0.02.
The reference program's roundings to bfloat16 on the way (of `normed`, `signal`, `jacobian`, `centered` and `weights`) count: a program that leaves them out, or rounds other values in their place, can miss the bound.
Values may be sent and summed in bfloat16 or wider, within the bound.
A program may use at most 64 MiB of HBM per device.

```python
import math
import jax
import jax.numpy as jnp
from jax import lax

D = 1024
FF = 4096
SITES = 256
LEVELS = 4
SAMPLES = 64


def place_ends(result, rng, smallest, high):
    dims = result.shape
    spot = [jax.random.randint(jax.random.fold_in(rng, axis), (), 0, dims[axis]) for axis in range(len(dims))]
    result = result.at[tuple(spot)].set(smallest)
    longest = dims.index(max(dims))
    spot[longest] = (spot[longest] + 1) % dims[longest]
    return result.at[tuple(spot)].set(high)


def steps_of(stream_key, dims, split, low, largest):
    def one(axis_at, parts):
        steps = jax.random.uniform(jax.random.fold_in(jax.random.fold_in(stream_key, 6), axis_at), (parts,), jnp.float32, low / len(split), largest / len(split))
        return jnp.repeat(jnp.exp(steps), dims[axis_at] // parts).reshape((-1,) + (1,) * (len(dims) - axis_at - 1))

    loudness = one(*split[0])
    for cut in split[1:]:
        loudness = loudness * one(*cut)
    return loudness


def bell_draw(rng, dims, scale, limit, shards=(), kind=jnp.bfloat16):
    drawn = scale * jax.random.normal(rng, dims, jnp.float32)
    if shards:
        drawn = drawn * steps_of(rng, dims, shards, -0.22, 0.18)
    return jnp.clip(drawn, -limit, limit).astype(kind)


def setup_inputs(seed: int = 0) -> dict:
    streams_of = jax.random.split(jax.random.key(seed), 7)
    hidden = bell_draw(streams_of[0], (SAMPLES, SITES, D), 1.0, 6.0, ((0, 64),))
    configs = place_ends(jax.random.randint(streams_of[1], (SAMPLES, SITES), 0, LEVELS), jax.random.fold_in(streams_of[1], 1), 0, LEVELS - 1).astype(jnp.int32)
    embed = bell_draw(streams_of[2], (LEVELS, D), 1.0, 6.0)
    w_up = bell_draw(streams_of[3], (D, FF), D ** -0.5, 0.1875, ((1, 8),))
    readout = bell_draw(streams_of[4], (FF,), 1.0, 6.0, ((0, 8),), jnp.float32)
    energies = bell_draw(streams_of[5], (SAMPLES,), 2.0, 12.0, ((0, 64),), jnp.float32)
    return {"hidden": hidden, "configs": configs, "embed": embed, "w_up": w_up, "readout": readout, "energies": energies}


norm_eps = 1e-06
diag_shift = 0.1

def features(hidden, configs, embed):
    levels = embed.shape[0]
    onehot = (configs[:, :, None] == jnp.arange(levels, dtype=jnp.int32)).astype(jnp.float32)
    added = jnp.einsum('sto,od->std', onehot, embed.astype(jnp.float32))
    summed = hidden.astype(jnp.float32) + added
    scale = lax.rsqrt(lax.optimization_barrier(jnp.mean(summed * summed, axis=-1, keepdims=True)) + norm_eps)
    return (summed * scale).astype(jnp.bfloat16)

def slope_of(preact):
    sigma = jax.nn.sigmoid(preact)
    return sigma * (1.0 + preact * (1.0 - sigma))

def solve_weights(gram, energy_all):
    count = gram.shape[0]
    trace_mean = jnp.trace(gram) / count
    system = gram + diag_shift * trace_mean * jnp.eye(count, dtype=gram.dtype)
    factor = jnp.linalg.cholesky(system)
    centered_e = (energy_all - jnp.mean(energy_all)) / math.sqrt(count)
    weights = jax.scipy.linalg.cho_solve((factor, True), centered_e)
    return (weights.astype(jnp.bfloat16), trace_mean)

def reference(hidden, configs, embed, w_up, readout, energies):
    normed = features(hidden, configs, embed)
    normed_wide = normed.astype(jnp.float32)
    block_width = min(FF, 512)
    block_count = FF // block_width
    w_blocks = w_up.reshape(D, block_count, block_width).transpose(1, 0, 2)
    r_blocks = readout.reshape(block_count, block_width)

    def one_block(pair):
        w_block, r_block = pair
        preact = jnp.einsum('std,df->stf', normed_wide, w_block.astype(jnp.float32))
        signal = (r_block * slope_of(preact)).astype(jnp.bfloat16)
        jacobian = jnp.einsum('std,stf->sdf', normed_wide, signal.astype(jnp.float32)).astype(jnp.bfloat16)
        flat = jacobian.reshape(SAMPLES, -1).astype(jnp.float32)
        mean_row = lax.optimization_barrier(jnp.mean(flat, axis=0))
        centered = ((flat - mean_row) / math.sqrt(SAMPLES)).astype(jnp.bfloat16)
        wide = centered.astype(jnp.float32)
        return (jnp.dot(wide, wide.T, precision=lax.Precision.HIGHEST), centered)
    partials, centered_all = lax.map(one_block, (w_blocks, r_blocks))
    gram = lax.optimization_barrier(jnp.sum(partials, axis=0))
    weights, trace_mean = solve_weights(gram, energies)
    weights_wide = weights.astype(jnp.float32)

    def update_block(centered):
        return jnp.dot(weights_wide, centered.astype(jnp.float32), precision=lax.Precision.HIGHEST)
    updates = lax.map(update_block, centered_all)
    update = updates.reshape(block_count, D, block_width).transpose(1, 0, 2).reshape(D, FF)
    return -trace_mean * update
```

```python
import functools

import jax
import jax.numpy as jnp
from jax import lax
from jax.experimental import pallas as pl
from jax.experimental.pallas import tpu as pltpu
from jax.sharding import PartitionSpec as P

norm_eps = 1e-06
diag_shift = 0.1
MESH = pl.DeviceIdType.MESH
COUNT = 64
ROWS = 16
NT = (((1,), (1,)), ((), ()))


def place():
    s = lax.axis_index("samp")
    p = lax.axis_index("par")
    return s // 32, (s // 4) % 8, s % 4, p // 2, p % 2


def samp_of(zh, y, x):
    return (zh * 8 + y) * 4 + x


def slope_of(z):
    sigma = 1.0 / (1.0 + jnp.exp(-z))
    return sigma * (1.0 + z * (1.0 - sigma))


def kernel(
    hidden, configs, embed, w_up, readout, energy, out,
    normed_t, jac, recv, cent, flat, part, buf_a, buf_b, buf_c, buf_d, scale,
    send_sem, recv_sem, ar_send, ar_recv,
):
    zh, y, x, zl, c = place()
    me = samp_of(zh, y, x)
    mypar = zl * 2 + c
    z = zh * 4 + zl
    slot_a = x * 2 + c

    barrier = pltpu.get_barrier_semaphore()

    def greet(d, carry):
        t = lax.rem(me + d, COUNT)
        pl.semaphore_signal(barrier, inc=1, device_id=(t, mypar), device_id_type=MESH)
        return carry

    lax.fori_loop(1, COUNT, greet, 0)
    for dx in range(4):
        pl.semaphore_signal(
            barrier, inc=1,
            device_id=(samp_of(zh, y, (x + dx) % 4), zl * 2 + (1 - c)), device_id_type=MESH)
    for dz in (1, 2, 3, 5, 6, 7):
        zt = (z + dz) % 8
        pl.semaphore_signal(
            barrier, inc=1,
            device_id=(samp_of(zt // 4, y, x), (zt % 4) * 2 + c), device_id_type=MESH)

    cfg = jnp.broadcast_to(configs[...].astype(jnp.float32), (8, 256)).T[:, 0:1]
    added = jnp.zeros((256, 1024), jnp.float32)
    for level in range(4):
        row = embed[level:level + 1, :].astype(jnp.float32)
        added = jnp.where(cfg == float(level), row, added)
    summed = hidden[0].astype(jnp.float32) + added
    norm = lax.rsqrt(jnp.mean(summed * summed, axis=-1, keepdims=True) + norm_eps)
    wide = summed * norm
    normed = wide.astype(jnp.bfloat16)
    normed_t[...] = normed.T
    preact = jnp.dot(normed, w_up[...], preferred_element_type=jnp.float32)
    signal = (readout[...] * slope_of(preact)).astype(jnp.bfloat16)

    def piece(dz, dq):
        yq = (y // 2 + dq) % 4
        zt = (zh + dz) % 2
        base = pl.multiple_of(samp_of(zt, yq * 2, 0) * ROWS, 128)
        block = jnp.dot(normed_t[pl.ds(base, 128), :], signal, preferred_element_type=jnp.float32)
        jac[pl.ds(base, 128), :] = block.astype(jnp.bfloat16)
        return zt, yq

    def send(zt, yq, dr, dx):
        t = samp_of(zt, yq * 2 + (y + dr) % 2, (x + dx) % 4)
        pltpu.make_async_remote_copy(
            src_ref=jac.at[pl.ds(pl.multiple_of(t * ROWS, ROWS), ROWS)],
            dst_ref=recv.at[me],
            send_sem=send_sem,
            recv_sem=recv_sem,
            device_id=(t, mypar),
            device_id_type=MESH,
        ).start()

    order = [(dr, dx) for dx in (0, 1, 3, 2) for dr in (0, 1)]
    zt, yq = piece(0, 0)
    pl.semaphore_wait(barrier, 73)
    for dr, dx in order[1:]:
        send(zt, yq, dr, dx)
    recv[me] = jac[pl.ds(pl.multiple_of(me * ROWS, ROWS), ROWS), :]

    def later(n, carry):
        zt, yq = piece(n % 2, n // 2)
        for dr, dx in order:
            send(zt, yq, dr, dx)
        return carry

    lax.fori_loop(1, 8, later, 0)

    pltpu.make_async_copy(recv.at[pl.ds(0, 63)], recv.at[pl.ds(0, 63)], recv_sem).wait()

    def add(s, total):
        return total + recv[s].astype(jnp.float32)

    total = lax.fori_loop(0, COUNT, add, jnp.zeros((ROWS, 512), jnp.float32), unroll=8)
    mean = total * (1.0 / COUNT)

    def center(s, carry):
        v = ((recv[s].astype(jnp.float32) - mean) * 0.125).astype(jnp.bfloat16)
        for j in range(4):
            cent[j, pl.ds(pl.multiple_of(s * ROWS, ROWS), ROWS), :] = (
                v[:, j * 128:(j + 1) * 128].astype(jnp.float32))
        return carry

    lax.fori_loop(0, COUNT, center, 0, unroll=8)

    for i in range(ROWS):
        for j in range(4):
            at = (i * 4 + j) * 128
            flat[:, at:at + 128] = cent[j, pl.ds(i, COUNT, stride=ROWS), :].astype(jnp.bfloat16)
    gram = lax.dot_general(flat[...], flat[...], NT, preferred_element_type=jnp.float32)
    rows = lax.broadcasted_iota(jnp.int32, (COUNT, COUNT), 0)
    lanes = lax.broadcasted_iota(jnp.int32, (COUNT, COUNT), 1)
    side = jnp.where((rows == me) & (lanes == 0), energy[0] * 0.125, 0.0)
    part[...] = jnp.concatenate([gram, side], axis=1).reshape(8, 8, 128)

    def exchange(buf, n, slot, src_of, target_of, own):
        copies = []
        for d in range(1, n):
            copy = pltpu.make_async_remote_copy(
                src_ref=src_of(d), dst_ref=buf.at[slot],
                send_sem=ar_send.at[own], recv_sem=ar_recv.at[own],
                device_id=target_of(d), device_id_type=MESH)
            copy.start()
        return copies

    def settle(buf, own):
        pltpu.make_async_copy(buf.at[pl.ds(0, 7)], buf.at[pl.ds(0, 7)], ar_recv.at[own]).wait()

    def settle_send(buf, own):
        pltpu.make_async_copy(buf.at[pl.ds(0, 7)], buf.at[pl.ds(0, 7)], ar_send.at[own]).wait()

    def peer_a(d):
        xt = (x + d // 2) % 4
        ct = (c + d) % 2
        return xt, ct

    def src_a(d):
        xt, ct = peer_a(d)
        return part.at[xt * 2 + ct]

    def dev_a(d):
        xt, ct = peer_a(d)
        return (samp_of(zh, y, xt), zl * 2 + ct)

    def dev_b(d):
        return (samp_of(zh, (y + d) % 8, x), mypar)

    def dev_c(d):
        zt = (z + d) % 8
        return (samp_of(zt // 4, y, x), (zt % 4) * 2 + c)

    exchange(buf_a, 8, slot_a, src_a, dev_a, 0)
    buf_a[slot_a] = part[slot_a]
    settle(buf_a, 0)
    buf_b[y] = jnp.sum(buf_a[...], axis=0)
    exchange(buf_b, 8, y, lambda d: buf_b.at[y], dev_b, 1)
    settle(buf_b, 1)
    buf_c[z] = jnp.sum(buf_b[...], axis=0)
    exchange(buf_c, 8, z, lambda d: buf_c.at[z], dev_c, 2)
    settle(buf_c, 2)
    buf_d[slot_a] = jnp.sum(buf_c[...], axis=0)
    exchange(buf_d, 8, slot_a, lambda d: buf_d.at[slot_a], dev_a, 3)
    settle(buf_d, 3)

    full = buf_d[...].reshape(COUNT, 128)
    row = lax.broadcasted_iota(jnp.int32, (COUNT, 128), 0)
    lane = lax.broadcasted_iota(jnp.int32, (COUNT, 128), 1)
    diag = row == lane
    trace_mean = jnp.sum(jnp.where(diag, full, 0.0), keepdims=True) * (1.0 / COUNT)
    right = lane == COUNT
    mean_e = jnp.sum(jnp.where(right, full, 0.0), keepdims=True) * (1.0 / COUNT)
    m = jnp.where(right, (full - mean_e) * 0.125, full + jnp.where(diag, diag_shift * trace_mean, 0.0))
    for k in range(COUNT):
        pivot = m[k:k + 1, :] * (1.0 / m[k:k + 1, k:k + 1])
        m = jnp.where(row == k, pivot, m - m[:, k:k + 1] * pivot)
    weights = m[:, COUNT:COUNT + 1].astype(jnp.bfloat16).astype(jnp.float32)
    scale[...] = jnp.broadcast_to(weights, (COUNT, 128))

    def apply(s, acc):
        w = scale[pl.ds(s, 1), :]
        at = pl.ds(pl.multiple_of(s * ROWS, ROWS), ROWS)
        return tuple(a + w * cent[j, at, :] for j, a in enumerate(acc))

    zero = jnp.zeros((ROWS, 128), jnp.float32)
    applied = lax.fori_loop(0, COUNT, apply, (zero,) * 4, unroll=8)
    for j in range(4):
        out[:, j * 128:(j + 1) * 128] = -trace_mean * applied[j]

    pltpu.make_async_copy(recv.at[pl.ds(0, 63)], recv.at[pl.ds(0, 63)], send_sem).wait()
    for own, buf in enumerate((buf_a, buf_b, buf_c, buf_d)):
        settle_send(buf, own)


def shards(hidden, configs, embed, w_up, readout, energies):
    vmem = pl.BlockSpec(memory_space=pltpu.VMEM)
    smem = pl.BlockSpec(memory_space=pltpu.SMEM)
    tile = pltpu.VMEM((8, 8, 128), jnp.float32)
    return pl.pallas_call(
        kernel,
        out_shape=jax.ShapeDtypeStruct((ROWS, 512), jnp.float32),
        in_specs=[vmem, vmem, vmem, vmem, vmem, smem],
        out_specs=vmem,
        scratch_shapes=[
            pltpu.VMEM((1024, 256), jnp.bfloat16),
            pltpu.VMEM((1024, 512), jnp.bfloat16),
            pltpu.VMEM((COUNT, ROWS, 512), jnp.bfloat16),
            pltpu.VMEM((4, COUNT * ROWS, 128), jnp.float32),
            pltpu.VMEM((COUNT, 8192), jnp.bfloat16),
            tile, tile, tile, tile, tile,
            pltpu.VMEM((COUNT, 128), jnp.float32),
            pltpu.SemaphoreType.DMA,
            pltpu.SemaphoreType.DMA,
            pltpu.SemaphoreType.DMA((4,)),
            pltpu.SemaphoreType.DMA((4,)),
        ],
        compiler_params=pltpu.CompilerParams(
            collective_id=0, has_side_effects=True, vmem_limit_bytes=48 << 20),
        name="step",
    )(hidden, configs, embed, w_up, readout.reshape(1, 512), energies)


def solution(mesh):
    in_specs = (P("samp", None, None), P("samp", None), P(), P(None, "par"), P("par"), P("samp"))
    out_specs = P("samp", "par")
    return jax.shard_map(shards, mesh=mesh, in_specs=in_specs, out_specs=out_specs, check_vma=False)
```

```python
import functools

import jax
import jax.numpy as jnp
from jax import lax
from jax.experimental import pallas as pl
from jax.experimental.pallas import tpu as pltpu
from jax.sharding import PartitionSpec as P

norm_eps = 1e-06
diag_shift = 0.1
MESH = pl.DeviceIdType.MESH
COUNT = 64
ROWS = 16
HALF = 32
PANEL = 8
NT = (((1,), (1,)), ((), ()))


def place():
    s = lax.axis_index("samp")
    p = lax.axis_index("par")
    return s // 32, (s // 4) % 8, s % 4, p // 2, p % 2


def samp_of(zh, y, x):
    return (zh * 8 + y) * 4 + x


def slope_of(z):
    sigma = 1.0 / (1.0 + jnp.exp(-z))
    return sigma * (1.0 + z * (1.0 - sigma))


def kernel(
    hidden_in, configs_in, embed_in, w_in, readout_in, energy_in, out,
    hidden, configs, embed, w_up, readout, energy,
    normed_t, jac, recv, cent, flat, buf_a, buf_b, buf_c, scale,
    in_sem, send_sem, recv_sem, ar_send, ar_recv,
):
    zh, y, x, zl, c = place()
    me = samp_of(zh, y, x)
    mypar = zl * 2 + c
    z = zh * 4 + zl
    slot_a = x * 2 + c

    barrier = pltpu.get_barrier_semaphore()

    def greet(d, carry):
        t = lax.rem(me + d, COUNT)
        pl.semaphore_signal(barrier, inc=1, device_id=(t, mypar), device_id_type=MESH)
        return carry

    lax.fori_loop(1, COUNT, greet, 0)
    for dx in range(4):
        pl.semaphore_signal(
            barrier, inc=1,
            device_id=(samp_of(zh, y, (x + dx) % 4), zl * 2 + (1 - c)), device_id_type=MESH)
    for dz in (1, 2, 3, 5, 6, 7):
        zt = (z + dz) % 8
        pl.semaphore_signal(
            barrier, inc=1,
            device_id=(samp_of(zt // 4, y, x), (zt % 4) * 2 + c), device_id_type=MESH)

    loads = [
        pltpu.make_async_copy(src, dst, in_sem.at[n])
        for n, (src, dst) in enumerate((
            (configs_in, configs), (embed_in, embed), (hidden_in, hidden),
            (readout_in, readout), (w_in, w_up), (energy_in, energy)))
    ]
    for load in loads:
        load.start()
    for load in loads[:3]:
        load.wait()

    cfg = jnp.broadcast_to(configs[...].astype(jnp.float32), (8, 256)).T[:, 0:1]
    added = jnp.zeros((256, 1024), jnp.float32)
    for level in range(4):
        row = embed[level:level + 1, :].astype(jnp.float32)
        added = jnp.where(cfg == float(level), row, added)
    summed = hidden[...].astype(jnp.float32) + added
    norm = lax.rsqrt(jnp.mean(summed * summed, axis=-1, keepdims=True) + norm_eps)
    wide = summed * norm
    normed = wide.astype(jnp.bfloat16)
    normed_t[...] = normed.T
    for load in loads[3:]:
        load.wait()
    preact = jnp.dot(normed, w_up[...], preferred_element_type=jnp.float32)
    signal = (readout[...] * slope_of(preact)).astype(jnp.bfloat16)

    def piece(dz, dq):
        yq = (y // 2 + dq) % 4
        zt = (zh + dz) % 2
        base = pl.multiple_of(samp_of(zt, yq * 2, 0) * ROWS, 128)
        block = jnp.dot(normed_t[pl.ds(base, 128), :], signal, preferred_element_type=jnp.float32)
        jac[pl.ds(base, 128), :] = block.astype(jnp.bfloat16)
        return zt, yq

    def send(zt, yq, dr, dx):
        t = samp_of(zt, yq * 2 + (y + dr) % 2, (x + dx) % 4)
        pltpu.make_async_remote_copy(
            src_ref=jac.at[pl.ds(pl.multiple_of(t * ROWS, ROWS), ROWS)],
            dst_ref=recv.at[me],
            send_sem=send_sem,
            recv_sem=recv_sem,
            device_id=(t, mypar),
            device_id_type=MESH,
        ).start()

    order = [(dr, dx) for dx in (0, 1, 3, 2) for dr in (0, 1)]
    zt, yq = piece(0, 0)
    pl.semaphore_wait(barrier, 73)
    for dr, dx in order[1:]:
        send(zt, yq, dr, dx)
    recv[me] = jac[pl.ds(pl.multiple_of(me * ROWS, ROWS), ROWS), :]

    def later(n, carry):
        zt, yq = piece(n % 2, n // 2)
        for dr, dx in order:
            send(zt, yq, dr, dx)
        return carry

    lax.fori_loop(1, 8, later, 0)

    pltpu.make_async_copy(recv.at[pl.ds(0, 63)], recv.at[pl.ds(0, 63)], recv_sem).wait()

    def add(s, total):
        return total + recv[s].astype(jnp.float32)

    total = lax.fori_loop(0, COUNT, add, jnp.zeros((ROWS, 512), jnp.float32), unroll=8)
    mean = total * (1.0 / COUNT)

    def center(s, carry):
        v = ((recv[s].astype(jnp.float32) - mean) * 0.125).astype(jnp.bfloat16)
        for j in range(4):
            cent[j, pl.ds(pl.multiple_of(s * ROWS, ROWS), ROWS), :] = (
                v[:, j * 128:(j + 1) * 128].astype(jnp.float32))
        return carry

    lax.fori_loop(0, COUNT, center, 0, unroll=8)

    for i in range(ROWS):
        for j in range(4):
            at = (i * 4 + j) * 128
            flat[:, at:at + 128] = cent[j, pl.ds(i, COUNT, stride=ROWS), :].astype(jnp.bfloat16)
    gram = lax.dot_general(flat[...], flat[...], NT, preferred_element_type=jnp.float32)
    up, left, low = gram[:HALF, :HALF], gram[HALF:, :HALF], gram[HALF:, HALF:]
    r32 = lax.broadcasted_iota(jnp.int32, (HALF, HALF), 0)
    c32 = lax.broadcasted_iota(jnp.int32, (HALF, HALF), 1)
    both = jnp.concatenate([jnp.where(c32 <= r32, up, low), left], axis=1)
    low_diag = jnp.sum(jnp.where(c32 == r32, low, 0.0), axis=0, keepdims=True)
    low_diag = jnp.concatenate([low_diag, jnp.zeros((1, 128 - HALF), jnp.float32)], axis=1)
    tail_row = lax.broadcasted_iota(jnp.int32, (8, 128), 0)
    tail_lane = lax.broadcasted_iota(jnp.int32, (8, 128), 1)
    mine = jnp.where((tail_row == 1) & (tail_lane == me), energy[...] * 0.125, 0.0)
    buf_a[slot_a, 0:16] = jnp.concatenate([both[:16], both[16:]], axis=1)
    buf_a[slot_a, 16:24] = jnp.where(tail_row == 0, low_diag, mine)

    def exchange(buf, slot, target_of, own):
        for d in range(1, 8):
            pltpu.make_async_remote_copy(
                src_ref=buf.at[slot], dst_ref=buf.at[slot],
                send_sem=ar_send.at[own], recv_sem=ar_recv.at[own],
                device_id=target_of(d), device_id_type=MESH).start()
        pltpu.make_async_copy(buf.at[pl.ds(0, 7)], buf.at[pl.ds(0, 7)], ar_recv.at[own]).wait()

    def settle_send(buf, own):
        pltpu.make_async_copy(buf.at[pl.ds(0, 7)], buf.at[pl.ds(0, 7)], ar_send.at[own]).wait()

    def dev_a(d):
        return (samp_of(zh, y, (x + d // 2) % 4), zl * 2 + (c + d) % 2)

    def dev_b(d):
        return (samp_of(zh, (y + d) % 8, x), mypar)

    def dev_c(d):
        zt = (z + d) % 8
        return (samp_of(zt // 4, y, x), (zt % 4) * 2 + c)

    exchange(buf_a, slot_a, dev_a, 0)
    buf_b[y] = jnp.sum(buf_a[...], axis=0)
    exchange(buf_b, y, dev_b, 1)
    buf_c[z] = jnp.sum(buf_b[...], axis=0)
    exchange(buf_c, z, dev_c, 2)
    whole = jnp.sum(buf_c[...], axis=0)

    both = jnp.concatenate([whole[:16, :COUNT], whole[:16, COUNT:]], axis=0)
    turned = jnp.concatenate([both, jnp.zeros((HALF, COUNT), jnp.float32)], axis=1).T
    mixed, mixed_t = both[:, :HALF], turned[:HALF]
    up = jnp.where(c32 <= r32, mixed, mixed_t)
    low = jnp.where(c32 > r32, mixed, jnp.where(c32 == r32, whole[16:17, :HALF], mixed_t))
    spare = jnp.zeros((HALF, COUNT), jnp.float32)
    full = jnp.concatenate([
        jnp.concatenate([up, turned[HALF:COUNT], spare], axis=1),
        jnp.concatenate([both[:, HALF:], low, spare], axis=1)], axis=0)
    energies = whole[17:18, :]
    row = lax.broadcasted_iota(jnp.int32, (COUNT, 128), 0)
    lane = lax.broadcasted_iota(jnp.int32, (COUNT, 128), 1)
    diag = row == lane
    trace_mean = jnp.sum(jnp.where(diag, full, 0.0), keepdims=True) * (1.0 / COUNT)
    mean_e = jnp.sum(energies, keepdims=True) * (1.0 / COUNT)
    rhs = jnp.sum(jnp.where(diag, (energies - mean_e) * 0.125, 0.0), axis=1, keepdims=True)
    m = jnp.where(lane == COUNT, rhs, full + jnp.where(diag, diag_shift * trace_mean, 0.0))
    for first in range(0, COUNT, PANEL):
        cols = [jnp.broadcast_to(m[:, k:k + 1], (COUNT, 128)) for k in range(first, first + PANEL)]
        for j in range(PANEL):
            k = first + j
            col = cols[j]
            inverse = 1.0 / col[k:k + 1, :]
            pivot = m[k:k + 1, :] * inverse
            m = jnp.where(row == k, pivot, m - col * pivot)
            for n in range(j + 1, PANEL):
                pivot = cols[n][k:k + 1, :] * inverse
                cols[n] = jnp.where(row == k, pivot, cols[n] - col * pivot)
    weights = m[:, COUNT:COUNT + 1].astype(jnp.bfloat16).astype(jnp.float32)
    scale[...] = jnp.broadcast_to(weights, (COUNT, 128))

    def apply(s, acc):
        w = scale[pl.ds(s, 1), :]
        at = pl.ds(pl.multiple_of(s * ROWS, ROWS), ROWS)
        return tuple(a + w * cent[j, at, :] for j, a in enumerate(acc))

    zero = jnp.zeros((ROWS, 128), jnp.float32)
    applied = lax.fori_loop(0, COUNT, apply, (zero,) * 4, unroll=8)
    for j in range(4):
        out[:, j * 128:(j + 1) * 128] = -trace_mean * applied[j]

    pltpu.make_async_copy(recv.at[pl.ds(0, 63)], recv.at[pl.ds(0, 63)], send_sem).wait()
    for own, buf in enumerate((buf_a, buf_b, buf_c)):
        settle_send(buf, own)


def shards(hidden, configs, embed, w_up, readout, energies):
    hbm = pl.BlockSpec(memory_space=pltpu.HBM)
    vmem = pl.BlockSpec(memory_space=pltpu.VMEM)
    args = (hidden[0], configs, embed, w_up, readout.reshape(1, 512), energies.reshape(1, 1))
    held = [pltpu.VMEM(a.shape, a.dtype) for a in args]
    sums = pltpu.VMEM((8, 24, 128), jnp.float32)
    return pl.pallas_call(
        kernel,
        out_shape=jax.ShapeDtypeStruct((ROWS, 512), jnp.float32),
        in_specs=[hbm] * 6,
        out_specs=vmem,
        scratch_shapes=held + [
            pltpu.VMEM((1024, 256), jnp.bfloat16),
            pltpu.VMEM((1024, 512), jnp.bfloat16),
            pltpu.VMEM((COUNT, ROWS, 512), jnp.bfloat16),
            pltpu.VMEM((4, COUNT * ROWS, 128), jnp.float32),
            pltpu.VMEM((COUNT, 8192), jnp.bfloat16),
            sums, sums, sums,
            pltpu.VMEM((COUNT, 128), jnp.float32),
            pltpu.SemaphoreType.DMA((6,)),
            pltpu.SemaphoreType.DMA,
            pltpu.SemaphoreType.DMA,
            pltpu.SemaphoreType.DMA((3,)),
            pltpu.SemaphoreType.DMA((3,)),
        ],
        compiler_params=pltpu.CompilerParams(
            collective_id=0, has_side_effects=True, vmem_limit_bytes=56 << 20),
        name="step",
    )(*args)


def solution(mesh):
    in_specs = (P("samp", None, None), P("samp", None), P(), P(None, "par"), P("par"), P("samp"))
    out_specs = P("samp", "par")
    return jax.shard_map(shards, mesh=mesh, in_specs=in_specs, out_specs=out_specs, check_vma=False)
```

```python
import functools

import jax
import jax.numpy as jnp
from jax import lax
from jax.experimental import pallas as pl
from jax.experimental.pallas import tpu as pltpu
from jax.sharding import PartitionSpec as P

norm_eps = 1e-06
diag_shift = 0.1
MESH = pl.DeviceIdType.MESH
COUNT = 64
ROWS = 16
HALF = 32
PANEL = 8
FAR = (4, 3, 5, 2, 6, 1, 7)
NT = (((1,), (1,)), ((), ()))


def place():
    s = lax.axis_index("samp")
    p = lax.axis_index("par")
    return s // 32, (s // 4) % 8, s % 4, p // 2, p % 2


def samp_of(zh, y, x):
    return (zh * 8 + y) * 4 + x


def slope_of(z):
    sigma = 1.0 / (1.0 + jnp.exp(-z))
    return sigma * (1.0 + z * (1.0 - sigma))


def kernel(
    hidden_in, configs_in, embed_in, w_in, readout_in, energy_in, out,
    hidden, configs, embed, w_up, readout, energy,
    normed_t, jac, recv, cent, flat, buf_a, buf_b, buf_c, scale,
    in_sem, send_sem, recv_sem, ar_send, ar_recv,
):
    zh, y, x, zl, c = place()
    me = samp_of(zh, y, x)
    mypar = zl * 2 + c
    z = zh * 4 + zl
    slot_a = x * 2 + c

    barrier = pltpu.get_barrier_semaphore()

    for dz in FAR:
        zt = (z + dz) % 8
        if dz == 4:
            continue
        pl.semaphore_signal(
            barrier, inc=1,
            device_id=(samp_of(zt // 4, y, x), (zt % 4) * 2 + c), device_id_type=MESH)

    ys = [(y + dy) % 8 for dy in FAR + (0,)]
    xs = [(x + dx) % 4 for dx in (2, 1, 3, 0)]
    for n, yt in enumerate(ys):
        for zt in (1 - zh, zh):
            line = (zt * 8 + yt) * 4
            for k, xt in enumerate(xs):
                if n == 7 and k == 3 and zt is zh:
                    continue
                pl.semaphore_signal(
                    barrier, inc=1, device_id=(line + xt, mypar), device_id_type=MESH)
    for dx in (2, 1, 3, 0):
        pl.semaphore_signal(
            barrier, inc=1,
            device_id=(samp_of(zh, y, (x + dx) % 4), zl * 2 + (1 - c)), device_id_type=MESH)

    loads = [
        pltpu.make_async_copy(src, dst, in_sem.at[n])
        for n, (src, dst) in enumerate((
            (configs_in, configs), (embed_in, embed), (hidden_in, hidden),
            (readout_in, readout), (w_in, w_up), (energy_in, energy)))
    ]
    for load in loads:
        load.start()
    for load in loads[:3]:
        load.wait()

    cfg = jnp.broadcast_to(configs[...].astype(jnp.float32), (8, 256)).T[:, 0:1]
    added = jnp.zeros((256, 1024), jnp.float32)
    for level in range(4):
        row = embed[level:level + 1, :].astype(jnp.float32)
        added = jnp.where(cfg == float(level), row, added)
    summed = hidden[...].astype(jnp.float32) + added
    norm = lax.rsqrt(jnp.mean(summed * summed, axis=-1, keepdims=True) + norm_eps)
    wide = summed * norm
    normed = wide.astype(jnp.bfloat16)
    normed_t[...] = normed.T
    for load in loads[3:]:
        load.wait()
    preact = jnp.dot(normed, w_up[...], preferred_element_type=jnp.float32)
    signal = (readout[...] * slope_of(preact)).astype(jnp.bfloat16)

    def piece(dz, dq):
        yq = (y // 2 + dq) % 4
        zt = (zh + dz) % 2
        base = pl.multiple_of(samp_of(zt, yq * 2, 0) * ROWS, 128)
        block = jnp.dot(normed_t[pl.ds(base, 128), :], signal, preferred_element_type=jnp.float32)
        jac[pl.ds(base, 128), :] = block.astype(jnp.bfloat16)
        return zt, yq

    def send(zt, yt, k):
        t = (zt * 8 + yt) * 4 + xs[k]
        pltpu.make_async_remote_copy(
            src_ref=jac.at[pl.ds(pl.multiple_of(t * ROWS, ROWS), ROWS)],
            dst_ref=recv.at[me],
            send_sem=send_sem,
            recv_sem=recv_sem,
            device_id=(t, mypar),
            device_id_type=MESH,
        ).start()

    sides = (y % 2, (y + 1) % 2)
    for n, (dz, dq) in enumerate(((1, 2), (0, 2), (1, 1), (0, 1), (1, 3), (0, 3), (1, 0), (0, 0))):
        zt, yq = piece(dz, dq)
        if n == 0:
            pl.semaphore_wait(barrier, 73)
        for k in range(4):
            for dr in (1, 0):
                if (dz, dq, k, dr) != (0, 0, 3, 0):
                    send(zt, yq * 2 + sides[dr], k)
    recv[me] = jac[pl.ds(pl.multiple_of(me * ROWS, ROWS), ROWS), :]

    pltpu.make_async_copy(recv.at[pl.ds(0, 63)], recv.at[pl.ds(0, 63)], recv_sem).wait()

    def add(s, total):
        return total + recv[s].astype(jnp.float32)

    total = lax.fori_loop(0, COUNT, add, jnp.zeros((ROWS, 512), jnp.float32), unroll=8)
    mean = total * (1.0 / COUNT)

    def center(s, carry):
        v = ((recv[s].astype(jnp.float32) - mean) * 0.125).astype(jnp.bfloat16)
        for j in range(4):
            cent[j, pl.ds(pl.multiple_of(s * ROWS, ROWS), ROWS), :] = (
                v[:, j * 128:(j + 1) * 128].astype(jnp.float32))
        return carry

    lax.fori_loop(0, COUNT, center, 0, unroll=8)

    for i in range(ROWS):
        for j in range(4):
            at = (i * 4 + j) * 128
            flat[:, at:at + 128] = cent[j, pl.ds(i, COUNT, stride=ROWS), :].astype(jnp.bfloat16)
    gram = lax.dot_general(flat[...], flat[...], NT, preferred_element_type=jnp.float32)
    up, left, low = gram[:HALF, :HALF], gram[HALF:, :HALF], gram[HALF:, HALF:]
    r32 = lax.broadcasted_iota(jnp.int32, (HALF, HALF), 0)
    c32 = lax.broadcasted_iota(jnp.int32, (HALF, HALF), 1)
    both = jnp.concatenate([jnp.where(c32 <= r32, up, low), left], axis=1)
    low_diag = jnp.sum(jnp.where(c32 == r32, low, 0.0), axis=0, keepdims=True)
    low_diag = jnp.concatenate([low_diag, jnp.zeros((1, 128 - HALF), jnp.float32)], axis=1)
    tail_row = lax.broadcasted_iota(jnp.int32, (8, 128), 0)
    tail_lane = lax.broadcasted_iota(jnp.int32, (8, 128), 1)
    mine = jnp.where((tail_row == 1) & (tail_lane == me), energy[...] * 0.125, 0.0)
    buf_a[slot_a, 0:16] = jnp.concatenate([both[:16], both[16:]], axis=1)
    buf_a[slot_a, 16:18] = jnp.where(tail_row == 0, low_diag, mine)[:2]

    def exchange(buf, slot, target_of, own, steps):
        for d in steps:
            pltpu.make_async_remote_copy(
                src_ref=buf.at[slot], dst_ref=buf.at[slot],
                send_sem=ar_send.at[own], recv_sem=ar_recv.at[own],
                device_id=target_of(d), device_id_type=MESH).start()
        pltpu.make_async_copy(buf.at[pl.ds(0, 7)], buf.at[pl.ds(0, 7)], ar_recv.at[own]).wait()

    def settle_send(buf, own):
        pltpu.make_async_copy(buf.at[pl.ds(0, 7)], buf.at[pl.ds(0, 7)], ar_send.at[own]).wait()

    def dev_a(d):
        return (samp_of(zh, y, (x + d // 2) % 4), zl * 2 + (c + d) % 2)

    def dev_b(d):
        return (samp_of(zh, (y + d) % 8, x), mypar)

    def dev_c(d):
        zt = (z + d) % 8
        return (samp_of(zt // 4, y, x), (zt % 4) * 2 + c)

    exchange(buf_a, slot_a, dev_a, 0, (1, 2, 3, 4, 5, 6, 7))
    buf_b[y] = jnp.sum(buf_a[...], axis=0)
    exchange(buf_b, y, dev_b, 1, range(1, 8))
    buf_c[z] = jnp.sum(buf_b[...], axis=0)
    exchange(buf_c, z, dev_c, 2, range(1, 8))
    whole = jnp.sum(buf_c[...], axis=0)

    both = jnp.concatenate([whole[:16, :COUNT], whole[:16, COUNT:]], axis=0)
    turned = jnp.concatenate([both, jnp.zeros((HALF, COUNT), jnp.float32)], axis=1).T
    mixed, mixed_t = both[:, :HALF], turned[:HALF]
    up = jnp.where(c32 <= r32, mixed, mixed_t)
    low = jnp.where(c32 > r32, mixed, jnp.where(c32 == r32, whole[16:17, :HALF], mixed_t))
    spare = jnp.zeros((HALF, COUNT), jnp.float32)
    full = jnp.concatenate([
        jnp.concatenate([up, turned[HALF:COUNT], spare], axis=1),
        jnp.concatenate([both[:, HALF:], low, spare], axis=1)], axis=0)
    energies = whole[17:18, :]
    row = lax.broadcasted_iota(jnp.int32, (COUNT, 128), 0)
    lane = lax.broadcasted_iota(jnp.int32, (COUNT, 128), 1)
    diag = row == lane
    trace_mean = jnp.sum(jnp.where(diag, full, 0.0), keepdims=True) * (1.0 / COUNT)
    mean_e = jnp.sum(energies, keepdims=True) * (1.0 / COUNT)
    rhs = jnp.sum(jnp.where(diag, (energies - mean_e) * 0.125, 0.0), axis=1, keepdims=True)
    m = jnp.where(lane == COUNT, rhs, full + jnp.where(diag, diag_shift * trace_mean, 0.0))
    for first in range(0, COUNT, PANEL):
        cols = [jnp.broadcast_to(m[:, k:k + 1], (COUNT, 128)) for k in range(first, first + PANEL)]
        for j in range(PANEL):
            k = first + j
            col = cols[j]
            inverse = 1.0 / col[k:k + 1, :]
            pivot = m[k:k + 1, :] * inverse
            m = jnp.where(row == k, pivot, m - col * pivot)
            for n in range(j + 1, PANEL):
                pivot = cols[n][k:k + 1, :] * inverse
                cols[n] = jnp.where(row == k, pivot, cols[n] - col * pivot)
    weights = m[:, COUNT:COUNT + 1].astype(jnp.bfloat16).astype(jnp.float32)
    scale[...] = jnp.broadcast_to(weights, (COUNT, 128))

    def apply(s, acc):
        w = scale[pl.ds(s, 1), :]
        at = pl.ds(pl.multiple_of(s * ROWS, ROWS), ROWS)
        return tuple(a + w * cent[j, at, :] for j, a in enumerate(acc))

    zero = jnp.zeros((ROWS, 128), jnp.float32)
    applied = lax.fori_loop(0, COUNT, apply, (zero,) * 4, unroll=8)
    for j in range(4):
        out[:, j * 128:(j + 1) * 128] = -trace_mean * applied[j]

    pltpu.make_async_copy(recv.at[pl.ds(0, 63)], recv.at[pl.ds(0, 63)], send_sem).wait()
    for own, buf in enumerate((buf_a, buf_b, buf_c)):
        settle_send(buf, own)


def shards(hidden, configs, embed, w_up, readout, energies):
    hbm = pl.BlockSpec(memory_space=pltpu.HBM)
    vmem = pl.BlockSpec(memory_space=pltpu.VMEM)
    args = (hidden[0], configs, embed, w_up, readout.reshape(1, 512), energies.reshape(1, 1))
    held = [pltpu.VMEM(a.shape, a.dtype) for a in args]
    sums = pltpu.VMEM((8, 18, 128), jnp.float32)
    return pl.pallas_call(
        kernel,
        out_shape=jax.ShapeDtypeStruct((ROWS, 512), jnp.float32),
        in_specs=[hbm] * 6,
        out_specs=vmem,
        scratch_shapes=held + [
            pltpu.VMEM((1024, 256), jnp.bfloat16),
            pltpu.VMEM((1024, 512), jnp.bfloat16),
            pltpu.VMEM((COUNT, ROWS, 512), jnp.bfloat16),
            pltpu.VMEM((4, COUNT * ROWS, 128), jnp.float32),
            pltpu.VMEM((COUNT, 8192), jnp.bfloat16),
            sums, sums, sums,
            pltpu.VMEM((COUNT, 128), jnp.float32),
            pltpu.SemaphoreType.DMA((6,)),
            pltpu.SemaphoreType.DMA,
            pltpu.SemaphoreType.DMA,
            pltpu.SemaphoreType.DMA((3,)),
            pltpu.SemaphoreType.DMA((3,)),
        ],
        compiler_params=pltpu.CompilerParams(
            collective_id=0, has_side_effects=True, vmem_limit_bytes=56 << 20),
        name="step",
    )(*args)


def solution(mesh):
    in_specs = (P("samp", None, None), P("samp", None), P(), P(None, "par"), P("par"), P("samp"))
    out_specs = P("samp", "par")
    return jax.shard_map(shards, mesh=mesh, in_specs=in_specs, out_specs=out_specs, check_vma=False)
```

```python
import functools

import jax
import jax.numpy as jnp
from jax import lax
from jax.experimental import pallas as pl
from jax.experimental.pallas import tpu as pltpu
from jax.sharding import PartitionSpec as P

norm_eps = 1e-06
diag_shift = 0.1
MESH = pl.DeviceIdType.MESH
COUNT = 64
ROWS = 16
HALF = 32
PANEL = 8
CUTS = (0, 384, 512)
FAR = (4, 3, 5, 2, 6, 1, 7)
NT = (((1,), (1,)), ((), ()))


def place():
    s = lax.axis_index("samp")
    p = lax.axis_index("par")
    return s // 32, (s // 4) % 8, s % 4, p // 2, p % 2


def samp_of(zh, y, x):
    return (zh * 8 + y) * 4 + x


def slope_of(z):
    sigma = 1.0 / (1.0 + jnp.exp(-z))
    return sigma * (1.0 + z * (1.0 - sigma))


def kernel(
    hidden_in, configs_in, embed_in, w_in, readout_in, energy_in, out,
    hidden, configs, embed, w_up, readout, energy,
    normed_t, jac_0, jac_1, recv_0, recv_1, cent, flat_0, flat_1, buf_a, buf_b, buf_c, scale,
    in_sem, send_sem, recv_sem, ar_send, ar_recv,
):
    jac, recv, flat = (jac_0, jac_1), (recv_0, recv_1), (flat_0, flat_1)
    zh, y, x, zl, c = place()
    me = samp_of(zh, y, x)
    mypar = zl * 2 + c
    z = zh * 4 + zl
    slot_a = x * 2 + c

    barrier = pltpu.get_barrier_semaphore()

    for dz in FAR:
        zt = (z + dz) % 8
        if dz == 4:
            continue
        pl.semaphore_signal(
            barrier, inc=1,
            device_id=(samp_of(zt // 4, y, x), (zt % 4) * 2 + c), device_id_type=MESH)

    ys = [(y + dy) % 8 for dy in FAR + (0,)]
    xs = [(x + dx) % 4 for dx in (2, 1, 3, 0)]
    for n, yt in enumerate(ys):
        for zt in (1 - zh, zh):
            line = (zt * 8 + yt) * 4
            for k, xt in enumerate(xs):
                if n == 7 and k == 3 and zt is zh:
                    continue
                pl.semaphore_signal(
                    barrier, inc=1, device_id=(line + xt, mypar), device_id_type=MESH)
    for dx in (2, 1, 3, 0):
        pl.semaphore_signal(
            barrier, inc=1,
            device_id=(samp_of(zh, y, (x + dx) % 4), zl * 2 + (1 - c)), device_id_type=MESH)

    loads = [
        pltpu.make_async_copy(src, dst, in_sem.at[n])
        for n, (src, dst) in enumerate((
            (configs_in, configs), (embed_in, embed), (hidden_in, hidden),
            (readout_in, readout), (w_in, w_up), (energy_in, energy)))
    ]
    for load in loads:
        load.start()
    for load in loads[:3]:
        load.wait()

    cfg = jnp.broadcast_to(configs[...].astype(jnp.float32), (8, 256)).T[:, 0:1]
    added = jnp.zeros((256, 1024), jnp.float32)
    for level in range(4):
        row = embed[level:level + 1, :].astype(jnp.float32)
        added = jnp.where(cfg == float(level), row, added)
    summed = hidden[...].astype(jnp.float32) + added
    norm = lax.rsqrt(jnp.mean(summed * summed, axis=-1, keepdims=True) + norm_eps)
    wide = summed * norm
    normed = wide.astype(jnp.bfloat16)
    normed_t[...] = normed.T
    for load in loads[3:]:
        load.wait()
    preact = jnp.dot(normed, w_up[...], preferred_element_type=jnp.float32)
    signal = (readout[...] * slope_of(preact)).astype(jnp.bfloat16)

    def piece(h, dz, dq):
        yq = (y // 2 + dq) % 4
        zt = (zh + dz) % 2
        base = pl.multiple_of(samp_of(zt, yq * 2, 0) * ROWS, 128)
        block = jnp.dot(
            normed_t[pl.ds(base, 128), :], signal[:, CUTS[h]:CUTS[h + 1]],
            preferred_element_type=jnp.float32)
        jac[h][pl.ds(base, 128), :] = block.astype(jnp.bfloat16)
        return zt, yq

    def send(h, zt, yt, k):
        t = (zt * 8 + yt) * 4 + xs[k]
        pltpu.make_async_remote_copy(
            src_ref=jac[h].at[pl.ds(pl.multiple_of(t * ROWS, ROWS), ROWS)],
            dst_ref=recv[h].at[me],
            send_sem=send_sem.at[h],
            recv_sem=recv_sem.at[h],
            device_id=(t, mypar),
            device_id_type=MESH,
        ).start()

    sides = (y % 2, (y + 1) % 2)
    steps = ((1, 2), (0, 1), (1, 3), (0, 2), (1, 1), (0, 3), (1, 0), (0, 0))
    for h in range(2):
        for n, (dz, dq) in enumerate(steps):
            zt, yq = piece(h, dz, dq)
            if h == 0 and n == 0:
                pl.semaphore_wait(barrier, 73)
            for k in range(4):
                for dr in (1, 0):
                    if (dz, dq, k, dr) != (0, 0, 3, 0):
                        send(h, zt, yq * 2 + sides[dr], k)
        recv[h][me] = jac[h][pl.ds(pl.multiple_of(me * ROWS, ROWS), ROWS), :]

    gram = jnp.zeros((COUNT, COUNT), jnp.float32)
    for h in range(2):
        first, blocks = CUTS[h] // 128, (CUTS[h + 1] - CUTS[h]) // 128
        got = recv[h].at[pl.ds(0, 63)]
        pltpu.make_async_copy(got, got, recv_sem.at[h]).wait()

        def add(s, total):
            return total + recv[h][s].astype(jnp.float32)

        total = lax.fori_loop(0, COUNT, add, jnp.zeros((ROWS, CUTS[h + 1] - CUTS[h]), jnp.float32), unroll=8)
        mean = total * (1.0 / COUNT)

        def center(s, carry):
            v = ((recv[h][s].astype(jnp.float32) - mean) * 0.125).astype(jnp.bfloat16)
            for j in range(blocks):
                cent[first + j, pl.ds(pl.multiple_of(s * ROWS, ROWS), ROWS), :] = (
                    v[:, j * 128:(j + 1) * 128].astype(jnp.float32))
            return carry

        lax.fori_loop(0, COUNT, center, 0, unroll=8)

        for i in range(ROWS):
            for j in range(blocks):
                at = (i * blocks + j) * 128
                flat[h][:, at:at + 128] = (
                    cent[first + j, pl.ds(i, COUNT, stride=ROWS), :].astype(jnp.bfloat16))
        gram += lax.dot_general(flat[h][...], flat[h][...], NT, preferred_element_type=jnp.float32)

    up, left, low = gram[:HALF, :HALF], gram[HALF:, :HALF], gram[HALF:, HALF:]
    r32 = lax.broadcasted_iota(jnp.int32, (HALF, HALF), 0)
    c32 = lax.broadcasted_iota(jnp.int32, (HALF, HALF), 1)
    both = jnp.concatenate([jnp.where(c32 <= r32, up, low), left], axis=1)
    low_diag = jnp.sum(jnp.where(c32 == r32, low, 0.0), axis=0, keepdims=True)
    low_diag = jnp.concatenate([low_diag, jnp.zeros((1, 128 - HALF), jnp.float32)], axis=1)
    tail_row = lax.broadcasted_iota(jnp.int32, (8, 128), 0)
    tail_lane = lax.broadcasted_iota(jnp.int32, (8, 128), 1)
    mine = jnp.where((tail_row == 1) & (tail_lane == me), energy[...] * 0.125, 0.0)
    buf_a[slot_a, 0:16] = jnp.concatenate([both[:16], both[16:]], axis=1)
    buf_a[slot_a, 16:18] = jnp.where(tail_row == 0, low_diag, mine)[:2]

    def exchange(buf, slot, target_of, own, steps):
        for d in steps:
            pltpu.make_async_remote_copy(
                src_ref=buf.at[slot], dst_ref=buf.at[slot],
                send_sem=ar_send.at[own], recv_sem=ar_recv.at[own],
                device_id=target_of(d), device_id_type=MESH).start()
        pltpu.make_async_copy(buf.at[pl.ds(0, 7)], buf.at[pl.ds(0, 7)], ar_recv.at[own]).wait()

    def settle_send(buf, own):
        pltpu.make_async_copy(buf.at[pl.ds(0, 7)], buf.at[pl.ds(0, 7)], ar_send.at[own]).wait()

    def dev_a(d):
        return (samp_of(zh, y, (x + d // 2) % 4), zl * 2 + (c + d) % 2)

    def dev_b(d):
        return (samp_of(zh, (y + d) % 8, x), mypar)

    def dev_c(d):
        zt = (z + d) % 8
        return (samp_of(zt // 4, y, x), (zt % 4) * 2 + c)

    exchange(buf_a, slot_a, dev_a, 0, (1, 2, 3, 4, 5, 6, 7))
    buf_b[y] = jnp.sum(buf_a[...], axis=0)
    exchange(buf_b, y, dev_b, 1, range(1, 8))
    buf_c[z] = jnp.sum(buf_b[...], axis=0)
    exchange(buf_c, z, dev_c, 2, range(1, 8))
    whole = jnp.sum(buf_c[...], axis=0)

    both = jnp.concatenate([whole[:16, :COUNT], whole[:16, COUNT:]], axis=0)
    turned = jnp.concatenate([both, jnp.zeros((HALF, COUNT), jnp.float32)], axis=1).T
    mixed, mixed_t = both[:, :HALF], turned[:HALF]
    up = jnp.where(c32 <= r32, mixed, mixed_t)
    low = jnp.where(c32 > r32, mixed, jnp.where(c32 == r32, whole[16:17, :HALF], mixed_t))
    spare = jnp.zeros((HALF, COUNT), jnp.float32)
    full = jnp.concatenate([
        jnp.concatenate([up, turned[HALF:COUNT], spare], axis=1),
        jnp.concatenate([both[:, HALF:], low, spare], axis=1)], axis=0)
    energies = whole[17:18, :]
    row = lax.broadcasted_iota(jnp.int32, (COUNT, 128), 0)
    lane = lax.broadcasted_iota(jnp.int32, (COUNT, 128), 1)
    diag = row == lane
    trace_mean = jnp.sum(jnp.where(diag, full, 0.0), keepdims=True) * (1.0 / COUNT)
    mean_e = jnp.sum(energies, keepdims=True) * (1.0 / COUNT)
    rhs = jnp.sum(jnp.where(diag, (energies - mean_e) * 0.125, 0.0), axis=1, keepdims=True)
    m = jnp.where(lane == COUNT, rhs, full + jnp.where(diag, diag_shift * trace_mean, 0.0))
    for first in range(0, COUNT, PANEL):
        cols = [jnp.broadcast_to(m[:, k:k + 1], (COUNT, 128)) for k in range(first, first + PANEL)]
        for j in range(PANEL):
            k = first + j
            col = cols[j]
            inverse = 1.0 / col[k:k + 1, :]
            pivot = m[k:k + 1, :] * inverse
            m = jnp.where(row == k, pivot, m - col * pivot)
            for n in range(j + 1, PANEL):
                pivot = cols[n][k:k + 1, :] * inverse
                cols[n] = jnp.where(row == k, pivot, cols[n] - col * pivot)
    weights = m[:, COUNT:COUNT + 1].astype(jnp.bfloat16).astype(jnp.float32)
    scale[...] = jnp.broadcast_to(weights, (COUNT, 128))

    def apply(s, acc):
        w = scale[pl.ds(s, 1), :]
        at = pl.ds(pl.multiple_of(s * ROWS, ROWS), ROWS)
        return tuple(a + w * cent[j, at, :] for j, a in enumerate(acc))

    zero = jnp.zeros((ROWS, 128), jnp.float32)
    applied = lax.fori_loop(0, COUNT, apply, (zero,) * 4, unroll=8)
    for j in range(4):
        out[:, j * 128:(j + 1) * 128] = -trace_mean * applied[j]

    for h in range(2):
        sent = recv[h].at[pl.ds(0, 63)]
        pltpu.make_async_copy(sent, sent, send_sem.at[h]).wait()
    for own, buf in enumerate((buf_a, buf_b, buf_c)):
        settle_send(buf, own)


def shards(hidden, configs, embed, w_up, readout, energies):
    hbm = pl.BlockSpec(memory_space=pltpu.HBM)
    vmem = pl.BlockSpec(memory_space=pltpu.VMEM)
    args = (hidden[0], configs, embed, w_up, readout.reshape(1, 512), energies.reshape(1, 1))
    held = [pltpu.VMEM(a.shape, a.dtype) for a in args]
    widths = (CUTS[1], CUTS[2] - CUTS[1])
    sums = pltpu.VMEM((8, 18, 128), jnp.float32)
    return pl.pallas_call(
        kernel,
        out_shape=jax.ShapeDtypeStruct((ROWS, 512), jnp.float32),
        in_specs=[hbm] * 6,
        out_specs=vmem,
        scratch_shapes=held + [
            pltpu.VMEM((1024, 256), jnp.bfloat16),
            *[pltpu.VMEM((1024, w), jnp.bfloat16) for w in widths],
            *[pltpu.VMEM((COUNT, ROWS, w), jnp.bfloat16) for w in widths],
            pltpu.VMEM((4, COUNT * ROWS, 128), jnp.float32),
            *[pltpu.VMEM((COUNT, ROWS * w), jnp.bfloat16) for w in widths],
            sums, sums, sums,
            pltpu.VMEM((COUNT, 128), jnp.float32),
            pltpu.SemaphoreType.DMA((6,)),
            pltpu.SemaphoreType.DMA((2,)),
            pltpu.SemaphoreType.DMA((2,)),
            pltpu.SemaphoreType.DMA((3,)),
            pltpu.SemaphoreType.DMA((3,)),
        ],
        compiler_params=pltpu.CompilerParams(
            collective_id=0, has_side_effects=True, vmem_limit_bytes=56 << 20),
        name="step",
    )(*args)


def solution(mesh):
    in_specs = (P("samp", None, None), P("samp", None), P(), P(None, "par"), P("par"), P("samp"))
    out_specs = P("samp", "par")
    return jax.shard_map(shards, mesh=mesh, in_specs=in_specs, out_specs=out_specs, check_vma=False)
```

```python
import functools

import jax
import jax.numpy as jnp
from jax import lax
from jax.experimental import pallas as pl
from jax.experimental.pallas import tpu as pltpu
from jax.sharding import PartitionSpec as P

norm_eps = 1e-06
diag_shift = 0.1
MESH = pl.DeviceIdType.MESH
COUNT = 64
ROWS = 16
HALF = 32
PANEL = 8
CUTS = (0, 384, 512)
FAR = (4, 3, 5, 2, 6, 1, 7)
NT = (((1,), (1,)), ((), ()))


def place():
    s = lax.axis_index("samp")
    p = lax.axis_index("par")
    return s // 32, (s // 4) % 8, s % 4, p // 2, p % 2


def samp_of(zh, y, x):
    return (zh * 8 + y) * 4 + x


def slope_of(z):
    sigma = 1.0 / (1.0 + jnp.exp(-z))
    return sigma * (1.0 + z * (1.0 - sigma))


def kernel(
    hidden_in, configs_in, embed_in, w_in, readout_in, energy_in, out,
    hidden, configs, embed, w_up, readout, energy,
    normed_t, jac_0, jac_1, recv_0, recv_1, cent, flat_0, flat_1, buf_a, buf_b, buf_c, scale,
    in_sem, send_sem, recv_sem, ar_send, ar_recv,
):
    jac, recv, flat = (jac_0, jac_1), (recv_0, recv_1), (flat_0, flat_1)
    zh, y, x, zl, c = place()
    me = samp_of(zh, y, x)
    mypar = zl * 2 + c
    z = zh * 4 + zl
    slot_a = x * 2 + c

    barrier = pltpu.get_barrier_semaphore()

    ys = [(y + dy) % 8 for dy in FAR + (0,)]
    xs = [(x + dx) % 4 for dx in (2, 1, 3, 0)]
    for n, yt in enumerate(ys):
        for zt in (1 - zh, zh):
            line = (zt * 8 + yt) * 4
            for k, xt in enumerate(xs):
                if n == 7 and k == 3 and zt is zh:
                    continue
                pl.semaphore_signal(
                    barrier, inc=1, device_id=(line + xt, mypar), device_id_type=MESH)
    for dx in (2, 1, 3, 0):
        pl.semaphore_signal(
            barrier, inc=1,
            device_id=(samp_of(zh, y, (x + dx) % 4), zl * 2 + (1 - c)), device_id_type=MESH)

    for dz in FAR:
        zt = (z + dz) % 8
        if dz == 4:
            continue
        pl.semaphore_signal(
            barrier, inc=1,
            device_id=(samp_of(zt // 4, y, x), (zt % 4) * 2 + c), device_id_type=MESH)

    loads = [
        pltpu.make_async_copy(src, dst, in_sem.at[n])
        for n, (src, dst) in enumerate((
            (configs_in, configs), (embed_in, embed), (hidden_in, hidden),
            (readout_in, readout), (w_in, w_up), (energy_in, energy)))
    ]
    for load in loads:
        load.start()
    for load in loads[:3]:
        load.wait()

    cfg = jnp.broadcast_to(configs[...].astype(jnp.float32), (8, 256)).T[:, 0:1]
    added = jnp.zeros((256, 1024), jnp.float32)
    for level in range(4):
        row = embed[level:level + 1, :].astype(jnp.float32)
        added = jnp.where(cfg == float(level), row, added)
    summed = hidden[...].astype(jnp.float32) + added
    norm = lax.rsqrt(jnp.mean(summed * summed, axis=-1, keepdims=True) + norm_eps)
    wide = summed * norm
    normed = wide.astype(jnp.bfloat16)
    normed_t[...] = normed.T
    for load in loads[3:]:
        load.wait()

    def signal_of(h):
        span = slice(CUTS[h], CUTS[h + 1])
        preact = jnp.dot(normed, w_up[:, span], preferred_element_type=jnp.float32)
        return (readout[:, span] * slope_of(preact)).astype(jnp.bfloat16)

    def piece(h, signal, dz, dq):
        yq = (y // 2 + dq) % 4
        zt = (zh + dz) % 2
        base = pl.multiple_of(samp_of(zt, yq * 2, 0) * ROWS, 128)
        block = jnp.dot(
            normed_t[pl.ds(base, 128), :], signal,
            preferred_element_type=jnp.float32)
        jac[h][pl.ds(base, 128), :] = block.astype(jnp.bfloat16)
        return zt, yq

    def send(h, zt, yt, k):
        t = (zt * 8 + yt) * 4 + xs[k]
        pltpu.make_async_remote_copy(
            src_ref=jac[h].at[pl.ds(pl.multiple_of(t * ROWS, ROWS), ROWS)],
            dst_ref=recv[h].at[me],
            send_sem=send_sem.at[h],
            recv_sem=recv_sem.at[h],
            device_id=(t, mypar),
            device_id_type=MESH,
        ).start()

    sides = (y % 2, (y + 1) % 2)
    steps = ((1, 2), (0, 1), (1, 3), (0, 2), (1, 1), (0, 3), (1, 0), (0, 0))
    for h in range(2):
        signal = signal_of(h)
        for n, (dz, dq) in enumerate(steps):
            zt, yq = piece(h, signal, dz, dq)
            if h == 0 and n == 0:
                pl.semaphore_wait(barrier, 73)
            for k in range(4):
                for dr in (1, 0):
                    if (dz, dq, k, dr) != (0, 0, 3, 0):
                        send(h, zt, yq * 2 + sides[dr], k)
        recv[h][me] = jac[h][pl.ds(pl.multiple_of(me * ROWS, ROWS), ROWS), :]

    gram = jnp.zeros((COUNT, COUNT), jnp.float32)
    for h in range(2):
        first, blocks = CUTS[h] // 128, (CUTS[h + 1] - CUTS[h]) // 128
        got = recv[h].at[pl.ds(0, 63)]
        pltpu.make_async_copy(got, got, recv_sem.at[h]).wait()

        def add(s, total):
            return total + recv[h][s].astype(jnp.float32)

        total = lax.fori_loop(0, COUNT, add, jnp.zeros((ROWS, CUTS[h + 1] - CUTS[h]), jnp.float32), unroll=16)
        mean = total * (1.0 / COUNT)

        def center(s, carry):
            v = ((recv[h][s].astype(jnp.float32) - mean) * 0.125).astype(jnp.bfloat16)
            for j in range(blocks):
                cent[first + j, pl.ds(pl.multiple_of(s * ROWS, ROWS), ROWS), :] = (
                    v[:, j * 128:(j + 1) * 128].astype(jnp.float32))
            return carry

        lax.fori_loop(0, COUNT, center, 0, unroll=16)

        for i in range(ROWS):
            for j in range(blocks):
                at = (i * blocks + j) * 128
                flat[h][:, at:at + 128] = (
                    cent[first + j, pl.ds(i, COUNT, stride=ROWS), :].astype(jnp.bfloat16))
        gram += lax.dot_general(flat[h][...], flat[h][...], NT, preferred_element_type=jnp.float32)

    up, left, low = gram[:HALF, :HALF], gram[HALF:, :HALF], gram[HALF:, HALF:]
    r32 = lax.broadcasted_iota(jnp.int32, (HALF, HALF), 0)
    c32 = lax.broadcasted_iota(jnp.int32, (HALF, HALF), 1)
    both = jnp.concatenate([jnp.where(c32 <= r32, up, low), left], axis=1)
    low_diag = jnp.sum(jnp.where(c32 == r32, low, 0.0), axis=0, keepdims=True)
    low_diag = jnp.concatenate([low_diag, jnp.zeros((1, 128 - HALF), jnp.float32)], axis=1)
    tail_row = lax.broadcasted_iota(jnp.int32, (8, 128), 0)
    tail_lane = lax.broadcasted_iota(jnp.int32, (8, 128), 1)
    mine = jnp.where((tail_row == 1) & (tail_lane == me), energy[...] * 0.125, 0.0)
    buf_a[slot_a, 0:16] = jnp.concatenate([both[:16], both[16:]], axis=1)
    buf_a[slot_a, 16:18] = jnp.where(tail_row == 0, low_diag, mine)[:2]

    def exchange(buf, slot, target_of, own, steps):
        for d in steps:
            pltpu.make_async_remote_copy(
                src_ref=buf.at[slot], dst_ref=buf.at[slot],
                send_sem=ar_send.at[own], recv_sem=ar_recv.at[own],
                device_id=target_of(d), device_id_type=MESH).start()
        pltpu.make_async_copy(buf.at[pl.ds(0, 7)], buf.at[pl.ds(0, 7)], ar_recv.at[own]).wait()

    def settle_send(buf, own):
        pltpu.make_async_copy(buf.at[pl.ds(0, 7)], buf.at[pl.ds(0, 7)], ar_send.at[own]).wait()

    def dev_a(d):
        return (samp_of(zh, y, (x + d // 2) % 4), zl * 2 + (c + d) % 2)

    def dev_b(d):
        return (samp_of(zh, (y + d) % 8, x), mypar)

    def dev_c(d):
        zt = (z + d) % 8
        return (samp_of(zt // 4, y, x), (zt % 4) * 2 + c)

    exchange(buf_a, slot_a, dev_a, 0, (1, 2, 3, 4, 5, 6, 7))
    buf_b[y] = jnp.sum(buf_a[...], axis=0)
    exchange(buf_b, y, dev_b, 1, range(1, 8))
    buf_c[z] = jnp.sum(buf_b[...], axis=0)
    exchange(buf_c, z, dev_c, 2, range(1, 8))
    whole = jnp.sum(buf_c[...], axis=0)

    both = jnp.concatenate([whole[:16, :COUNT], whole[:16, COUNT:]], axis=0)
    turned = jnp.concatenate([both, jnp.zeros((HALF, COUNT), jnp.float32)], axis=1).T
    mixed, mixed_t = both[:, :HALF], turned[:HALF]
    up = jnp.where(c32 <= r32, mixed, mixed_t)
    low = jnp.where(c32 > r32, mixed, jnp.where(c32 == r32, whole[16:17, :HALF], mixed_t))
    spare = jnp.zeros((HALF, COUNT), jnp.float32)
    full = jnp.concatenate([
        jnp.concatenate([up, turned[HALF:COUNT], spare], axis=1),
        jnp.concatenate([both[:, HALF:], low, spare], axis=1)], axis=0)
    energies = whole[17:18, :]
    row = lax.broadcasted_iota(jnp.int32, (COUNT, 128), 0)
    lane = lax.broadcasted_iota(jnp.int32, (COUNT, 128), 1)
    diag = row == lane
    trace_mean = jnp.sum(jnp.where(diag, full, 0.0), keepdims=True) * (1.0 / COUNT)
    mean_e = jnp.sum(energies, keepdims=True) * (1.0 / COUNT)
    rhs = jnp.sum(jnp.where(diag, (energies - mean_e) * 0.125, 0.0), axis=1, keepdims=True)
    m = jnp.where(lane == COUNT, rhs, full + jnp.where(diag, diag_shift * trace_mean, 0.0))
    for first in range(0, COUNT, PANEL):
        cols = [jnp.broadcast_to(m[:, k:k + 1], (COUNT, 128)) for k in range(first, first + PANEL)]
        for j in range(PANEL):
            k = first + j
            col = cols[j]
            inverse = 1.0 / col[k:k + 1, :]
            pivot = m[k:k + 1, :] * inverse
            m = jnp.where(row == k, pivot, m - col * pivot)
            for n in range(j + 1, PANEL):
                pivot = cols[n][k:k + 1, :] * inverse
                cols[n] = jnp.where(row == k, pivot, cols[n] - col * pivot)
    weights = m[:, COUNT:COUNT + 1].astype(jnp.bfloat16).astype(jnp.float32)
    scale[...] = jnp.broadcast_to(weights, (COUNT, 128))

    def apply(s, acc):
        w = scale[pl.ds(s, 1), :]
        at = pl.ds(pl.multiple_of(s * ROWS, ROWS), ROWS)
        return tuple(a + w * cent[j, at, :] for j, a in enumerate(acc))

    zero = jnp.zeros((ROWS, 128), jnp.float32)
    applied = lax.fori_loop(0, COUNT, apply, (zero,) * 4, unroll=16)
    for j in range(4):
        out[:, j * 128:(j + 1) * 128] = -trace_mean * applied[j]

    for h in range(2):
        sent = recv[h].at[pl.ds(0, 63)]
        pltpu.make_async_copy(sent, sent, send_sem.at[h]).wait()
    for own, buf in enumerate((buf_a, buf_b, buf_c)):
        settle_send(buf, own)


def shards(hidden, configs, embed, w_up, readout, energies):
    hbm = pl.BlockSpec(memory_space=pltpu.HBM)
    vmem = pl.BlockSpec(memory_space=pltpu.VMEM)
    args = (hidden[0], configs, embed, w_up, readout.reshape(1, 512), energies.reshape(1, 1))
    held = [pltpu.VMEM(a.shape, a.dtype) for a in args]
    widths = (CUTS[1], CUTS[2] - CUTS[1])
    sums = pltpu.VMEM((8, 18, 128), jnp.float32)
    return pl.pallas_call(
        kernel,
        out_shape=jax.ShapeDtypeStruct((ROWS, 512), jnp.float32),
        in_specs=[hbm] * 6,
        out_specs=vmem,
        scratch_shapes=held + [
            pltpu.VMEM((1024, 256), jnp.bfloat16),
            *[pltpu.VMEM((1024, w), jnp.bfloat16) for w in widths],
            *[pltpu.VMEM((COUNT, ROWS, w), jnp.bfloat16) for w in widths],
            pltpu.VMEM((4, COUNT * ROWS, 128), jnp.float32),
            *[pltpu.VMEM((COUNT, ROWS * w), jnp.bfloat16) for w in widths],
            sums, sums, sums,
            pltpu.VMEM((COUNT, 128), jnp.float32),
            pltpu.SemaphoreType.DMA((6,)),
            pltpu.SemaphoreType.DMA((2,)),
            pltpu.SemaphoreType.DMA((2,)),
            pltpu.SemaphoreType.DMA((3,)),
            pltpu.SemaphoreType.DMA((3,)),
        ],
        compiler_params=pltpu.CompilerParams(
            collective_id=0, has_side_effects=True, vmem_limit_bytes=56 << 20),
        name="step",
    )(*args)


def solution(mesh):
    in_specs = (P("samp", None, None), P("samp", None), P(), P(None, "par"), P("par"), P("samp"))
    out_specs = P("samp", "par")
    return jax.shard_map(shards, mesh=mesh, in_specs=in_specs, out_specs=out_specs, check_vma=False)
```

```python
import functools

import jax
import jax.numpy as jnp
from jax import lax
from jax.experimental import pallas as pl
from jax.experimental.pallas import tpu as pltpu
from jax.sharding import PartitionSpec as P

norm_eps = 1e-06
diag_shift = 0.1
MESH = pl.DeviceIdType.MESH
COUNT = 64
ROWS = 16
HALF = 32
PANEL = 8
CUTS = (0, 384, 512)
FAR = (4, 3, 5, 2, 6, 1, 7)
NT = (((1,), (1,)), ((), ()))


def place():
    s = lax.axis_index("samp")
    p = lax.axis_index("par")
    return s // 32, (s // 4) % 8, s % 4, p // 2, p % 2


def samp_of(zh, y, x):
    return (zh * 8 + y) * 4 + x


def slope_of(z):
    sigma = 1.0 / (1.0 + jnp.exp(-z))
    return sigma * (1.0 + z * (1.0 - sigma))


def kernel(
    hidden_in, configs_in, embed_in, w_in, readout_in, energy_in, out,
    hidden, configs, embed, w_up, readout, energy,
    normed_t, jac_0, jac_1, recv_0, recv_1, cent, flat_0, flat_1, buf_k, buf_a, buf_b, buf_c, scale,
    in_sem, send_sem, recv_sem, ar_send, ar_recv,
):
    jac, recv, flat = (jac_0, jac_1), (recv_0, recv_1), (flat_0, flat_1)
    zh, y, x, zl, c = place()
    me = samp_of(zh, y, x)
    mypar = zl * 2 + c
    z = zh * 4 + zl

    barrier = pltpu.get_barrier_semaphore()

    for dz in FAR:
        zt = (z + dz) % 8
        if dz == 4:
            continue
        pl.semaphore_signal(
            barrier, inc=1,
            device_id=(samp_of(zt // 4, y, x), (zt % 4) * 2 + c), device_id_type=MESH)

    ys = [(y + dy) % 8 for dy in FAR + (0,)]
    xs = [(x + dx) % 4 for dx in (2, 1, 3, 0)]
    for n, yt in enumerate(ys):
        for zt in (1 - zh, zh):
            line = (zt * 8 + yt) * 4
            for k, xt in enumerate(xs):
                if n == 7 and k == 3 and zt is zh:
                    continue
                pl.semaphore_signal(
                    barrier, inc=1, device_id=(line + xt, mypar), device_id_type=MESH)
    pl.semaphore_signal(
        barrier, inc=1, device_id=(me, zl * 2 + 1 - c), device_id_type=MESH)

    loads = [
        pltpu.make_async_copy(src, dst, in_sem.at[n])
        for n, (src, dst) in enumerate((
            (configs_in, configs), (embed_in, embed), (hidden_in, hidden),
            (readout_in, readout), (w_in, w_up), (energy_in, energy)))
    ]
    for load in loads:
        load.start()
    for load in loads[:3]:
        load.wait()

    cfg = jnp.broadcast_to(configs[...].astype(jnp.float32), (8, 256)).T[:, 0:1]
    added = jnp.zeros((256, 1024), jnp.float32)
    for level in range(4):
        row = embed[level:level + 1, :].astype(jnp.float32)
        added = jnp.where(cfg == float(level), row, added)
    summed = hidden[...].astype(jnp.float32) + added
    norm = lax.rsqrt(jnp.mean(summed * summed, axis=-1, keepdims=True) + norm_eps)
    wide = summed * norm
    normed = wide.astype(jnp.bfloat16)
    normed_t[...] = normed.T
    for load in loads[3:]:
        load.wait()
    preact = jnp.dot(normed, w_up[...], preferred_element_type=jnp.float32)
    signal = (readout[...] * slope_of(preact)).astype(jnp.bfloat16)

    def piece(h, dz, dq):
        yq = (y // 2 + dq) % 4
        zt = (zh + dz) % 2
        base = pl.multiple_of(samp_of(zt, yq * 2, 0) * ROWS, 128)
        block = jnp.dot(
            normed_t[pl.ds(base, 128), :], signal[:, CUTS[h]:CUTS[h + 1]],
            preferred_element_type=jnp.float32)
        jac[h][pl.ds(base, 128), :] = block.astype(jnp.bfloat16)
        return zt, yq

    def send(h, zt, yt, k):
        t = (zt * 8 + yt) * 4 + xs[k]
        pltpu.make_async_remote_copy(
            src_ref=jac[h].at[pl.ds(pl.multiple_of(t * ROWS, ROWS), ROWS)],
            dst_ref=recv[h].at[me],
            send_sem=send_sem.at[h],
            recv_sem=recv_sem.at[h],
            device_id=(t, mypar),
            device_id_type=MESH,
        ).start()

    sides = (y % 2, (y + 1) % 2)
    steps = ((1, 2), (0, 1), (1, 3), (0, 2), (1, 1), (0, 3), (1, 0), (0, 0))
    for h in range(2):
        for n, (dz, dq) in enumerate(steps):
            zt, yq = piece(h, dz, dq)
            if h == 0 and n == 0:
                pl.semaphore_wait(barrier, 70)
            for k in range(4):
                for dr in (1, 0):
                    if (dz, dq, k, dr) != (0, 0, 3, 0):
                        send(h, zt, yq * 2 + sides[dr], k)
        recv[h][me] = jac[h][pl.ds(pl.multiple_of(me * ROWS, ROWS), ROWS), :]

    gram = jnp.zeros((COUNT, COUNT), jnp.float32)
    for h in range(2):
        first, blocks = CUTS[h] // 128, (CUTS[h + 1] - CUTS[h]) // 128
        got = recv[h].at[pl.ds(0, 63)]
        pltpu.make_async_copy(got, got, recv_sem.at[h]).wait()

        def add(s, total):
            return total + recv[h][s].astype(jnp.float32)

        total = lax.fori_loop(0, COUNT, add, jnp.zeros((ROWS, CUTS[h + 1] - CUTS[h]), jnp.float32), unroll=8)
        mean = total * (1.0 / COUNT)

        def center(s, carry):
            v = ((recv[h][s].astype(jnp.float32) - mean) * 0.125).astype(jnp.bfloat16)
            for j in range(blocks):
                cent[first + j, pl.ds(pl.multiple_of(s * ROWS, ROWS), ROWS), :] = (
                    v[:, j * 128:(j + 1) * 128].astype(jnp.float32))
            return carry

        lax.fori_loop(0, COUNT, center, 0, unroll=8)

        for i in range(ROWS):
            for j in range(blocks):
                at = (i * blocks + j) * 128
                flat[h][:, at:at + 128] = (
                    cent[first + j, pl.ds(i, COUNT, stride=ROWS), :].astype(jnp.bfloat16))
        gram += lax.dot_general(flat[h][...], flat[h][...], NT, preferred_element_type=jnp.float32)

    up, left, low = gram[:HALF, :HALF], gram[HALF:, :HALF], gram[HALF:, HALF:]
    r32 = lax.broadcasted_iota(jnp.int32, (HALF, HALF), 0)
    c32 = lax.broadcasted_iota(jnp.int32, (HALF, HALF), 1)
    both = jnp.concatenate([jnp.where(c32 <= r32, up, low), left], axis=1)
    low_diag = jnp.sum(jnp.where(c32 == r32, low, 0.0), axis=0, keepdims=True)
    low_diag = jnp.concatenate([low_diag, jnp.zeros((1, 128 - HALF), jnp.float32)], axis=1)
    tail_row = lax.broadcasted_iota(jnp.int32, (8, 128), 0)
    tail_lane = lax.broadcasted_iota(jnp.int32, (8, 128), 1)
    mine = jnp.where((tail_row == 1) & (tail_lane == me), energy[...] * 0.125, 0.0)
    buf_k[c, 0:16] = jnp.concatenate([both[:16], both[16:]], axis=1)
    buf_k[c, 16:18] = jnp.where(tail_row == 0, low_diag, mine)[:2]

    def exchange(buf, slot, target_of, own, steps):
        for d in steps:
            pltpu.make_async_remote_copy(
                src_ref=buf.at[slot], dst_ref=buf.at[slot],
                send_sem=ar_send.at[own], recv_sem=ar_recv.at[own],
                device_id=target_of(d), device_id_type=MESH).start()
        some = buf.at[pl.ds(0, buf.shape[0] - 1)]
        pltpu.make_async_copy(some, some, ar_recv.at[own]).wait()

    def settle_send(buf, own):
        some = buf.at[pl.ds(0, buf.shape[0] - 1)]
        pltpu.make_async_copy(some, some, ar_send.at[own]).wait()

    def dev_k(d):
        return (me, zl * 2 + 1 - c)

    def dev_a(d):
        return (samp_of(zh, y, (x + d) % 4), mypar)

    def dev_b(d):
        return (samp_of(zh, (y + d) % 8, x), mypar)

    def dev_c(d):
        zt = (z + d) % 8
        return (samp_of(zt // 4, y, x), (zt % 4) * 2 + c)

    exchange(buf_k, c, dev_k, 3, (1,))
    buf_a[x] = jnp.sum(buf_k[...], axis=0)
    exchange(buf_a, x, dev_a, 0, (2, 1, 3))
    buf_b[y] = jnp.sum(buf_a[...], axis=0)
    exchange(buf_b, y, dev_b, 1, range(1, 8))
    buf_c[z] = jnp.sum(buf_b[...], axis=0)
    exchange(buf_c, z, dev_c, 2, range(1, 8))
    whole = jnp.sum(buf_c[...], axis=0)

    both = jnp.concatenate([whole[:16, :COUNT], whole[:16, COUNT:]], axis=0)
    turned = jnp.concatenate([both, jnp.zeros((HALF, COUNT), jnp.float32)], axis=1).T
    mixed, mixed_t = both[:, :HALF], turned[:HALF]
    up = jnp.where(c32 <= r32, mixed, mixed_t)
    low = jnp.where(c32 > r32, mixed, jnp.where(c32 == r32, whole[16:17, :HALF], mixed_t))
    spare = jnp.zeros((HALF, COUNT), jnp.float32)
    full = jnp.concatenate([
        jnp.concatenate([up, turned[HALF:COUNT], spare], axis=1),
        jnp.concatenate([both[:, HALF:], low, spare], axis=1)], axis=0)
    energies = whole[17:18, :]
    row = lax.broadcasted_iota(jnp.int32, (COUNT, 128), 0)
    lane = lax.broadcasted_iota(jnp.int32, (COUNT, 128), 1)
    diag = row == lane
    trace_mean = jnp.sum(jnp.where(diag, full, 0.0), keepdims=True) * (1.0 / COUNT)
    mean_e = jnp.sum(energies, keepdims=True) * (1.0 / COUNT)
    rhs = jnp.sum(jnp.where(diag, (energies - mean_e) * 0.125, 0.0), axis=1, keepdims=True)
    m = jnp.where(lane == COUNT, rhs, full + jnp.where(diag, diag_shift * trace_mean, 0.0))
    for first in range(0, COUNT, PANEL):
        cols = [jnp.broadcast_to(m[:, k:k + 1], (COUNT, 128)) for k in range(first, first + PANEL)]
        for j in range(PANEL):
            k = first + j
            col = cols[j]
            inverse = 1.0 / col[k:k + 1, :]
            pivot = m[k:k + 1, :] * inverse
            m = jnp.where(row == k, pivot, m - col * pivot)
            for n in range(j + 1, PANEL):
                pivot = cols[n][k:k + 1, :] * inverse
                cols[n] = jnp.where(row == k, pivot, cols[n] - col * pivot)
    weights = m[:, COUNT:COUNT + 1].astype(jnp.bfloat16).astype(jnp.float32)
    scale[...] = jnp.broadcast_to(weights, (COUNT, 128))

    def apply(s, acc):
        w = scale[pl.ds(s, 1), :]
        at = pl.ds(pl.multiple_of(s * ROWS, ROWS), ROWS)
        return tuple(a + w * cent[j, at, :] for j, a in enumerate(acc))

    zero = jnp.zeros((ROWS, 128), jnp.float32)
    applied = lax.fori_loop(0, COUNT, apply, (zero,) * 4, unroll=8)
    for j in range(4):
        out[:, j * 128:(j + 1) * 128] = -trace_mean * applied[j]

    for h in range(2):
        sent = recv[h].at[pl.ds(0, 63)]
        pltpu.make_async_copy(sent, sent, send_sem.at[h]).wait()
    for own, buf in enumerate((buf_a, buf_b, buf_c, buf_k)):
        settle_send(buf, own)


def shards(hidden, configs, embed, w_up, readout, energies):
    hbm = pl.BlockSpec(memory_space=pltpu.HBM)
    vmem = pl.BlockSpec(memory_space=pltpu.VMEM)
    args = (hidden[0], configs, embed, w_up, readout.reshape(1, 512), energies.reshape(1, 1))
    held = [pltpu.VMEM(a.shape, a.dtype) for a in args]
    widths = (CUTS[1], CUTS[2] - CUTS[1])
    sums = pltpu.VMEM((8, 18, 128), jnp.float32)
    return pl.pallas_call(
        kernel,
        out_shape=jax.ShapeDtypeStruct((ROWS, 512), jnp.float32),
        in_specs=[hbm] * 6,
        out_specs=vmem,
        scratch_shapes=held + [
            pltpu.VMEM((1024, 256), jnp.bfloat16),
            *[pltpu.VMEM((1024, w), jnp.bfloat16) for w in widths],
            *[pltpu.VMEM((COUNT, ROWS, w), jnp.bfloat16) for w in widths],
            pltpu.VMEM((4, COUNT * ROWS, 128), jnp.float32),
            *[pltpu.VMEM((COUNT, ROWS * w), jnp.bfloat16) for w in widths],
            pltpu.VMEM((2, 18, 128), jnp.float32),
            pltpu.VMEM((4, 18, 128), jnp.float32),
            sums, sums,
            pltpu.VMEM((COUNT, 128), jnp.float32),
            pltpu.SemaphoreType.DMA((6,)),
            pltpu.SemaphoreType.DMA((2,)),
            pltpu.SemaphoreType.DMA((2,)),
            pltpu.SemaphoreType.DMA((4,)),
            pltpu.SemaphoreType.DMA((4,)),
        ],
        compiler_params=pltpu.CompilerParams(
            collective_id=0, has_side_effects=True, vmem_limit_bytes=56 << 20),
        name="step",
    )(*args)


def solution(mesh):
    in_specs = (P("samp", None, None), P("samp", None), P(), P(None, "par"), P("par"), P("samp"))
    out_specs = P("samp", "par")
    return jax.shard_map(shards, mesh=mesh, in_specs=in_specs, out_specs=out_specs, check_vma=False)
```
